32 devices in a mesh: head: 2 (over x), tm: 4 (over y, core), space: 4 (over z).
Axes of the slice: x: 2, y: 2, z: 4, core: 2. Of those that a mesh axis runs over, the one named last changes fastest.
Arguments:
- query_tiles: bfloat16 [4, 4, 4, 1, 384, 128], P('head', 'tm', 'space'), may hold values from -6 to 6
- key_tiles: bfloat16 [4, 4, 4, 1, 384, 128], P('head', 'tm', 'space'), may hold values from -6 to 6
- value_tiles: bfloat16 [4, 4, 4, 1, 384, 128], P('head', 'tm', 'space'), may hold values from -6 to 6
- out_tiles: bfloat16 [4, 4, 4, 1, 384, 128], P('head', 'tm', 'space'), may hold values from -6 to 6
- grad_tiles: bfloat16 [4, 4, 4, 1, 384, 128], P('head', 'tm', 'space'), may hold values from -6 to 6
- log_sum_exp: float32 [4, 4, 4, 1, 384], P('head', 'tm', 'space'), may hold values from 4 to 6
Outputs:
- grad_query: bfloat16 [4, 4, 4, 1, 384, 128], P('head', 'tm', 'space')
- grad_key: bfloat16 [4, 4, 4, 1, 384, 128], P('head', 'tm', 'space')
- grad_value: bfloat16 [4, 4, 4, 1, 384, 128], P('head', 'tm', 'space')
The draws below stay inside these ranges and needn't reach their ends.
All inputs are finite; a program needn't handle non-finite values.
Results may differ from the reference program's by a relative error of at most 0.0051.
Values may be sent and summed in bfloat16 or wider, within the bound.
A program may use at most 64 MiB of HBM per device.

```python
import jax
import jax.numpy as jnp
from jax import lax

HEADS = 4
DH = 128
TILE = 384
TC = 1
NT = 4
NR = 4


def shard_levels(rng, shape, split, smallest, largest):
    level = 1.0
    for position, parts in split:
        heights = jax.random.uniform(jax.random.fold_in(jax.random.fold_in(rng, 6), position), (parts,), jnp.float32, smallest / len(split), largest / len(split))
        level = level * jnp.repeat(jnp.exp(heights), shape[position] // parts).reshape((-1,) + (1,) * (len(shape) - 1 - position))
    return level


def bell_draw(rng, shape, deviation, most, shards=(), dtype=jnp.bfloat16):
    entries = jax.random.normal(rng, shape, jnp.float32) * deviation
    if len(shards) > 0:
        entries = shard_levels(rng, shape, shards, -0.22, 0.18) * entries
    return jnp.clip(entries, min=-most, max=most).astype(dtype)


def setup_inputs(seed: int = 0) -> dict:
    key_list = jax.random.split(jax.random.key(seed), 7)
    return {
        "query_tiles": bell_draw(key_list[0], (HEADS, NT, NR, TC, TILE, DH), 1.0, 6.0, ((0, 2), (1, 4), (2, 4))),
        "key_tiles": bell_draw(key_list[1], (HEADS, NT, NR, TC, TILE, DH), 1.0, 6.0, ((0, 2), (1, 4), (2, 4))),
        "value_tiles": bell_draw(key_list[2], (HEADS, NT, NR, TC, TILE, DH), 1.0, 6.0, ((0, 2), (1, 4), (2, 4))),
        "out_tiles": bell_draw(key_list[3], (HEADS, NT, NR, TC, TILE, DH), 1.0, 6.0, ((0, 2), (1, 4), (2, 4))),
        "grad_tiles": bell_draw(key_list[4], (HEADS, NT, NR, TC, TILE, DH), 1.0, 6.0, ((0, 2), (1, 4), (2, 4))),
        "log_sum_exp": jnp.clip(4.0 + 2.0 * jax.random.uniform(key_list[5], (HEADS, NT, NR, TC, TILE), jnp.float32) ** shard_levels(key_list[5], (HEADS, NT, NR, TC, TILE), ((0, 2), (1, 4), (2, 4)), -0.2, 0.2), 4.0, 6.0),
    }


def rounded(values):
    return lax.optimization_barrier(values.astype(jnp.bfloat16)).astype(jnp.float32)


def reference(query_tiles, key_tiles, value_tiles, out_tiles, grad_tiles, log_sum_exp):
    score_scale = query_tiles.shape[-1] ** -0.5
    row_delta = jnp.sum(grad_tiles.astype(jnp.float32) * out_tiles.astype(jnp.float32), axis=-1)
    frames, row_tiles, column_tiles = query_tiles.shape[1:4]
    present = jnp.pad(jnp.ones((frames, row_tiles, column_tiles), jnp.float32), 1)
    pad_width = ((1, 1), (1, 1), (1, 1), (0, 0), (0, 0))

    def one_head(packed):
        queries, keys_head, values_head, grads, lse_head, delta_head = packed
        queries = queries.astype(jnp.float32)
        grads = grads.astype(jnp.float32)
        keys_pad = jnp.pad(keys_head.astype(jnp.float32), pad_width)
        values_pad = jnp.pad(values_head.astype(jnp.float32), pad_width)
        grad_q = jnp.zeros(queries.shape, jnp.float32)
        key_acc = jnp.zeros(keys_pad.shape, jnp.float32)
        value_acc = jnp.zeros(keys_pad.shape, jnp.float32)
        for step_t in range(3):
            for step_r in range(3):
                for step_c in range(3):
                    window = (slice(step_t, step_t + frames), slice(step_r, step_r + row_tiles), slice(step_c, step_c + column_tiles))
                    keys_now = keys_pad[window]
                    values_now = values_pad[window]
                    mask_now = present[window][..., None, None]
                    scores = jnp.einsum("trcqd,trckd->trcqk", queries, keys_now) * score_scale
                    attention = jnp.exp(scores - lse_head[..., None]) * mask_now
                    dprob = jnp.einsum("trcqd,trckd->trcqk", grads, values_now)
                    dscore = attention * (dprob - delta_head[..., None])
                    attention_round = rounded(attention)
                    dscore_round = rounded(dscore)
                    grad_q = grad_q + jnp.einsum("trcqk,trckd->trcqd", dscore_round, keys_now) * score_scale
                    key_acc = key_acc.at[window].add(jnp.einsum("trcqk,trcqd->trckd", dscore_round, queries) * score_scale)
                    value_acc = value_acc.at[window].add(jnp.einsum("trcqk,trcqd->trckd", attention_round, grads))
        inner = (slice(1, -1), slice(1, -1), slice(1, -1))
        return grad_q, key_acc[inner], value_acc[inner]

    grad_q, grad_k, grad_v = lax.map(one_head, (query_tiles, key_tiles, value_tiles, grad_tiles, log_sum_exp, row_delta))
    return (grad_q.astype(jnp.bfloat16), grad_k.astype(jnp.bfloat16), grad_v.astype(jnp.bfloat16))
```

```python
import functools
import math

import jax
import jax.numpy as jnp
from jax import lax
from jax.experimental import pallas as pl
from jax.experimental.pallas import tpu as pltpu
from jax.sharding import PartitionSpec as P


MESH = pl.DeviceIdType.MESH
LOG2E = math.log2(math.e)
NT_DIMS = (((1,), (1,)), ((), ()))


def member(role, group):
    return 2 * group + lax.rem(role + group, 2)


def kernel(
    rows,
    q_ref, k_ref, v_ref, o_ref, g_ref, lse_ref,
    gq_ref, gk_ref, gv_ref,
    qbuf, gbuf, stat, kbuf, vbuf, kt, own_g, own_o, own_lse, own_stat,
    dq_acc, dk_acc, dv_acc, dq_send, dk_send, dv_send, dq_recv, dk_recv, dv_recv,
    lsem, s_own, s_near, s_cross, s_dq, s_dkv, r_q, r_kv, r_dq, r_dkv,
):
    tile, dim = q_ref.shape[1:]
    scale = dim ** -0.5
    t = lax.axis_index("tm")
    z = lax.axis_index("space")
    group = t // 2
    r = lax.rem(t + group, 2)
    other = 1 - r
    partner = member(other, group)
    has_low = z > 0
    has_high = z < rows - 1
    inner_there = member(1, 1 - group)

    def copy(src, dst, ssem, rsem, tm, space):
        return pltpu.make_async_remote_copy(
            src_ref=src, dst_ref=dst, send_sem=ssem, recv_sem=rsem,
            device_id={"tm": tm, "space": space}, device_id_type=MESH,
        )

    barrier = pltpu.get_barrier_semaphore()

    def greet(tm, space):
        pl.semaphore_signal(
            barrier, inc=1, device_id={"tm": tm, "space": space}, device_id_type=MESH
        )

    greet(partner, z)
    greet(inner_there, z)

    @pl.when(r == 1)
    def _():
        greet(member(0, 1 - group), z)

    @pl.when(has_low)
    def _():
        greet(t, z - 1)
        greet(partner, z - 1)

    @pl.when(has_high)
    def _():
        greet(t, z + 1)
        greet(partner, z + 1)

    local = [
        pltpu.make_async_copy(q_ref.at[r], qbuf.at[r], lsem.at[0]),
        pltpu.make_async_copy(k_ref.at[r], kbuf.at[r], lsem.at[1]),
        pltpu.make_async_copy(v_ref.at[r], vbuf.at[r], lsem.at[2]),
        pltpu.make_async_copy(g_ref.at[r], gbuf.at[r], lsem.at[3]),
        pltpu.make_async_copy(g_ref, own_g, lsem.at[4]),
        pltpu.make_async_copy(o_ref, own_o, lsem.at[5]),
        pltpu.make_async_copy(lse_ref, own_lse, lsem.at[6]),
    ]
    for c in local:
        c.start()

    low_n = has_low.astype(jnp.int32)
    high_n = has_high.astype(jnp.int32)
    pl.semaphore_wait(barrier, 2 + r + 2 * low_n + 2 * high_n)

    def near_copies(direction, k):
        head = r if k == 0 else other
        space = z + 1 if direction == 0 else z - 1
        tm = t if k == 0 else partner
        slot = 2 * (1 + direction) + r
        return [
            copy(src, dst.at[slot], s_near.at[direction, k, i], r_q.at[slot, i], tm, space)
            for i, (src, dst) in enumerate(
                ((q_ref.at[head], qbuf), (g_ref.at[head], gbuf), (own_stat.at[head], stat))
            )
        ]

    own_copies = [
        copy(q_ref.at[other], qbuf.at[r], s_own.at[0], r_q.at[r, 0], partner, z),
        copy(k_ref.at[other], kbuf.at[r], s_own.at[1], r_kv.at[r, 0], partner, z),
        copy(v_ref.at[other], vbuf.at[r], s_own.at[2], r_kv.at[r, 1], partner, z),
        copy(g_ref.at[other], gbuf.at[r], s_own.at[3], r_q.at[r, 1], partner, z),
        copy(own_stat.at[other], stat.at[r], s_own.at[4], r_q.at[r, 2], partner, z),
    ]

    def cross_copies():
        out = []
        for head in range(2):
            tm = member(head, 1 - group)
            out.append(copy(k_ref.at[head], kbuf.at[2], s_cross.at[head, 0], r_kv.at[2, 0], tm, z))
            out.append(copy(v_ref.at[head], vbuf.at[2], s_cross.at[head, 1], r_kv.at[2, 1], tm, z))
        return out

    for k in range(2):
        @pl.when(has_high)
        def _():
            for c in near_copies(0, k)[:2]:
                c.start()

        @pl.when(has_low)
        def _():
            for c in near_copies(1, k)[:2]:
                c.start()

        if k == 0:
            for c in own_copies[:4]:
                c.start()

            @pl.when(r == 1)
            def _():
                for c in cross_copies():
                    c.start()

    for c in local:
        c.wait()
    for head in range(2):
        prod = own_g[head].astype(jnp.float32) * own_o[head].astype(jnp.float32)
        own_stat[head, 0:1, :] = own_lse[head, 0, 0] * LOG2E
        own_stat[head, 1:2, :] = jnp.sum(prod.T, axis=0, keepdims=True)
    own_copies[4].start()
    for k in range(2):
        @pl.when(has_high)
        def _():
            near_copies(0, k)[2].start()

        @pl.when(has_low)
        def _():
            near_copies(1, k)[2].start()

    dq_acc[...] = jnp.zeros_like(dq_acc)
    dk_acc[...] = jnp.zeros_like(dk_acc)
    dv_acc[...] = jnp.zeros_like(dv_acc)
    stat[r] = own_stat[r]
    kt[r] = kbuf[r].T

    def pair(qs, ks):
        qb = qbuf[qs]
        gb = gbuf[qs]
        kb = kbuf[ks]
        vb = vbuf[ks]
        s = lax.dot_general(kb, qb, NT_DIMS, preferred_element_type=jnp.float32)
        p = jnp.exp2(s * (scale * LOG2E) - stat[qs, 0:1, :])
        dp = lax.dot_general(vb, gb, NT_DIMS, preferred_element_type=jnp.float32)
        ds = (p * (dp - stat[qs, 1:2, :])).astype(jnp.bfloat16)
        p = p.astype(jnp.bfloat16)
        dv_acc[ks] += jnp.dot(p, gb, preferred_element_type=jnp.float32)
        dk_acc[ks] += jnp.dot(ds, qb, preferred_element_type=jnp.float32)
        dq_acc[qs] += jnp.dot(kt[ks], ds, preferred_element_type=jnp.float32)

    def q_arrivals(slot):
        return [
            copy(q_ref.at[0], qbuf.at[slot], s_own.at[0], r_q.at[slot, 0], partner, z),
            copy(g_ref.at[0], gbuf.at[slot], s_own.at[0], r_q.at[slot, 1], partner, z),
            copy(own_stat.at[0], stat.at[slot], s_own.at[0], r_q.at[slot, 2], partner, z),
        ]

    def kv_arrivals(slot):
        return [
            copy(k_ref.at[0], kbuf.at[slot], s_own.at[0], r_kv.at[slot, 0], partner, z),
            copy(v_ref.at[0], vbuf.at[slot], s_own.at[0], r_kv.at[slot, 1], partner, z),
        ]

    @pl.loop(0, 4)
    def _(i):
        @pl.when(i == 1)
        def _():
            for c in q_arrivals(other) + kv_arrivals(other):
                c.wait_recv()
            kt[other] = kbuf[other].T

        pair(lax.rem(r + i // 2, 2), lax.rem(r + i, 2))

    for c in kv_arrivals(2):
        c.wait_recv()
    kt[2] = kbuf[2].T

    def dq_copy(slot, source, tm, space):
        return copy(
            dq_send.at[slot], dq_recv.at[r, source], s_dq.at[slot], r_dq.at[r, source], tm, space
        )

    def own_dq_copy():
        return dq_copy(other, 0, partner, z)

    def near_dq_copy(direction, role):
        space = z - 1 if direction == 0 else z + 1
        return dq_copy(2 * (1 + direction) + role, 2 - direction, member(role, group), space)

    def cross_dkv():
        return [
            copy(dk_send.at[2], dk_recv.at[r, 1], s_dkv.at[2, 0], r_dkv.at[r, 1, 0], inner_there, z),
            copy(dv_send.at[2], dv_recv.at[r, 1], s_dkv.at[2, 1], r_dkv.at[r, 1, 1], inner_there, z),
        ]

    def own_dkv():
        return [
            copy(dk_send.at[other], dk_recv.at[r, 0], s_dkv.at[other, 0], r_dkv.at[r, 0, 0], partner, z),
            copy(dv_send.at[other], dv_recv.at[r, 0], s_dkv.at[other, 1], r_dkv.at[r, 0, 1], partner, z),
        ]

    pair(1, 2)

    dq_send[other] = (dq_acc[other] * scale).astype(jnp.bfloat16)
    own_dq_copy().start()

    first = 1 - low_n
    last = 1 + high_n

    @pl.loop(0, 2)
    def _(step):
        role = lax.rem(r + step, 2)

        @pl.when(has_low)
        def _():
            for c in q_arrivals(2 + role):
                c.wait_recv()

        @pl.when(has_high)
        def _():
            for c in q_arrivals(4 + role):
                c.wait_recv()

        @pl.when(role == 1)
        def _():
            @pl.loop(first, last)
            def _(d):
                pair(2 * (1 + d) + 1, 2)

            dk_send[2] = (dk_acc[2] * scale).astype(jnp.bfloat16)
            dv_send[2] = dv_acc[2].astype(jnp.bfloat16)
            for c in cross_dkv():
                c.start()

        @pl.loop(2 * first, 2 * last)
        def _(i):
            d = i // 2
            slot = 2 * (1 + d) + role
            pair(slot, lax.rem(i, 2))

            @pl.when(lax.rem(i, 2) == 1)
            def _():
                dq_send[slot] = (dq_acc[slot] * scale).astype(jnp.bfloat16)

                @pl.when(d == 0)
                def _():
                    near_dq_copy(0, role).start()

                @pl.when(d == 1)
                def _():
                    near_dq_copy(1, role).start()

    dk_send[other] = (dk_acc[other] * scale).astype(jnp.bfloat16)
    dv_send[other] = dv_acc[other].astype(jnp.bfloat16)
    for c in own_dkv():
        c.start()

    def dq_arrival(head, source):
        return copy(
            dq_send.at[0], dq_recv.at[head, source], s_own.at[0], r_dq.at[head, source], partner, z
        )

    def dkv_arrivals(head, source):
        return [
            copy(dk_send.at[0], dk_recv.at[head, source], s_own.at[0], r_dkv.at[head, source, 0], partner, z),
            copy(dv_send.at[0], dv_recv.at[head, source], s_own.at[0], r_dkv.at[head, source, 1], partner, z),
        ]

    dk_mine = dk_acc[r] * scale
    dv_mine = dv_acc[r]

    @pl.when(r == 0)
    def _():
        gk_ref[r] = dk_mine.astype(gk_ref.dtype)
        gv_ref[r] = dv_mine.astype(gv_ref.dtype)
        for c in dkv_arrivals(other, 0):
            c.wait_recv()
        gk_ref[other] = dk_recv[other, 0]
        gv_ref[other] = dv_recv[other, 0]

    @pl.when(r == 1)
    def _():
        for c in dkv_arrivals(0, 1) + dkv_arrivals(1, 1):
            c.wait_recv()
        gk_ref[r] = (dk_mine + dk_recv[r, 1].astype(jnp.float32)).astype(gk_ref.dtype)
        gv_ref[r] = (dv_mine + dv_recv[r, 1].astype(jnp.float32)).astype(gv_ref.dtype)
        for c in dkv_arrivals(other, 0):
            c.wait_recv()
        for recv, out in ((dk_recv, gk_ref), (dv_recv, gv_ref)):
            out[other] = (
                recv[other, 0].astype(jnp.float32) + recv[other, 1].astype(jnp.float32)
            ).astype(out.dtype)

    dq_arrival(other, 0).wait_recv()
    totals = [dq_acc.at[r], dq_acc.at[other]]
    dq_acc[r] = dq_acc[r] * scale
    dq_acc[other] = dq_recv[other, 0].astype(jnp.float32)

    for source, there in ((1, has_low), (2, has_high)):
        @pl.when(there)
        def _():
            for head, total in ((r, totals[0]), (other, totals[1])):
                dq_arrival(head, source).wait_recv()
                total[...] += dq_recv[head, source].astype(jnp.float32)

    for head, total in ((r, totals[0]), (other, totals[1])):
        gq_ref[head] = total[...].T.astype(gq_ref.dtype)

    for c in own_copies + [own_dq_copy()] + cross_dkv() + own_dkv():
        c.wait_send()

    @pl.when(r == 1)
    def _():
        for c in cross_copies():
            c.wait_send()

    @pl.when(has_high)
    def _():
        for c in near_copies(0, 0) + near_copies(0, 1):
            c.wait_send()
        for role in range(2):
            near_dq_copy(1, role).wait_send()

    @pl.when(has_low)
    def _():
        for c in near_copies(1, 0) + near_copies(1, 1):
            c.wait_send()
        for role in range(2):
            near_dq_copy(0, role).wait_send()


def body(rows, query_tiles, key_tiles, value_tiles, out_tiles, grad_tiles, log_sum_exp):
    heads, _, _, columns, tile, dim = query_tiles.shape
    flat = (heads, tile, dim)
    bf, f32 = jnp.bfloat16, jnp.float32
    dma = pltpu.SemaphoreType.DMA
    outs = pl.pallas_call(
        functools.partial(kernel, rows),
        out_shape=[jax.ShapeDtypeStruct(flat, bf)] * 3,
        in_specs=[pl.BlockSpec(memory_space=pl.ANY)] * 6,
        out_specs=[pl.BlockSpec(memory_space=pltpu.VMEM)] * 3,
        scratch_shapes=[
            pltpu.VMEM((6, tile, dim), bf),
            pltpu.VMEM((6, tile, dim), bf),
            pltpu.VMEM((6, 2, tile), f32),
            pltpu.VMEM((3, tile, dim), bf),
            pltpu.VMEM((3, tile, dim), bf),
            pltpu.VMEM((3, dim, tile), bf),
            pltpu.VMEM(flat, bf),
            pltpu.VMEM(flat, bf),
            pltpu.VMEM((heads, 1, 1, 1, tile), f32),
            pltpu.VMEM((heads, 2, tile), f32),
            pltpu.VMEM((6, dim, tile), f32),
            pltpu.VMEM((3, tile, dim), f32),
            pltpu.VMEM((3, tile, dim), f32),
            pltpu.VMEM((6, dim, tile), bf),
            pltpu.VMEM((3, tile, dim), bf),
            pltpu.VMEM((3, tile, dim), bf),
            pltpu.VMEM((2, 3, dim, tile), bf),
            pltpu.VMEM((2, 2, tile, dim), bf),
            pltpu.VMEM((2, 2, tile, dim), bf),
            dma((7,)),
            dma((5,)),
            dma((2, 2, 3)),
            dma((2, 2)),
            dma((6,)),
            dma((3, 2)),
            dma((6, 3)),
            dma((3, 2)),
            dma((2, 3)),
            dma((2, 2, 2)),
        ],
        compiler_params=pltpu.CompilerParams(
            collective_id=0, has_side_effects=True, vmem_limit_bytes=40 * 2**20
        ),
        cost_estimate=pl.CostEstimate(
            flops=15 * 5 * 2 * tile * tile * dim,
            bytes_accessed=16 * tile * dim * 2,
            transcendentals=15 * tile * tile,
        ),
        name="tile_attention_backward",
    )(
        query_tiles.reshape(flat), key_tiles.reshape(flat), value_tiles.reshape(flat),
        out_tiles.reshape(flat), grad_tiles.reshape(flat), log_sum_exp,
    )
    return tuple(o.reshape(query_tiles.shape) for o in outs)


def solution(mesh):
    tiles = P("head", "tm", "space", None, None, None)
    assert mesh.shape["tm"] == 4
    return jax.shard_map(
        functools.partial(body, mesh.shape["space"]),
        mesh=mesh,
        in_specs=(tiles,) * 5 + (P("head", "tm", "space", None, None),),
        out_specs=(tiles,) * 3,
        check_vma=False,
    )
```

```python
import functools
import math

import jax
import jax.numpy as jnp
from jax import lax
from jax.experimental import pallas as pl
from jax.experimental.pallas import tpu as pltpu
from jax.sharding import PartitionSpec as P


MESH = pl.DeviceIdType.MESH
LOG2E = math.log2(math.e)
NT_DIMS = (((1,), (1,)), ((), ()))


def member(role, group):
    return 2 * group + lax.rem(role + group, 2)


def kernel(
    rows,
    q_ref, k_ref, v_ref, o_ref, g_ref, lse_ref,
    grads_ref,
    qbuf, gbuf, stat, kbuf, vbuf, kt, own_g, own_o, own_lse, own_stat,
    dq_acc, dk_acc, dv_acc, dq_send, dk_send, dv_send, dq_recv, dk_recv, dv_recv,
    lsem, s_own, s_near, s_cross, s_dq, s_dkv, r_q, r_kv, r_dq, r_dkv,
):
    tile, dim = q_ref.shape[1:]
    scale = dim ** -0.5
    t = lax.axis_index("tm")
    z = lax.axis_index("space")
    group = t // 2
    r = lax.rem(t + group, 2)
    other = 1 - r
    partner = member(other, group)
    has_low = z > 0
    has_high = z < rows - 1
    inner_there = member(1, 1 - group)

    def copy(src, dst, ssem, rsem, tm, space):
        return pltpu.make_async_remote_copy(
            src_ref=src, dst_ref=dst, send_sem=ssem, recv_sem=rsem,
            device_id={"tm": tm, "space": space}, device_id_type=MESH,
        )

    gq_ref, gk_ref, gv_ref = (grads_ref.at[i] for i in range(3))
    barrier = pltpu.get_barrier_semaphore()

    def greet(tm, space):
        pl.semaphore_signal(
            barrier, inc=1, device_id={"tm": tm, "space": space}, device_id_type=MESH
        )

    greet(partner, z)
    greet(inner_there, z)

    @pl.when(r == 1)
    def _():
        greet(member(0, 1 - group), z)

    @pl.when(has_low)
    def _():
        greet(t, z - 1)
        greet(partner, z - 1)

    @pl.when(has_high)
    def _():
        greet(t, z + 1)
        greet(partner, z + 1)

    local = [
        pltpu.make_async_copy(q_ref.at[r], qbuf.at[r], lsem.at[0]),
        pltpu.make_async_copy(k_ref.at[r], kbuf.at[r], lsem.at[1]),
        pltpu.make_async_copy(v_ref.at[r], vbuf.at[r], lsem.at[2]),
        pltpu.make_async_copy(g_ref.at[r], gbuf.at[r], lsem.at[3]),
        pltpu.make_async_copy(g_ref, own_g, lsem.at[4]),
        pltpu.make_async_copy(o_ref, own_o, lsem.at[5]),
        pltpu.make_async_copy(lse_ref, own_lse, lsem.at[6]),
    ]
    for c in local:
        c.start()

    low_n = has_low.astype(jnp.int32)
    high_n = has_high.astype(jnp.int32)
    pl.semaphore_wait(barrier, 2 + r + 2 * low_n + 2 * high_n)

    def near_copies(direction, k, parts=(0, 1, 2)):
        head = r if k == 0 else other
        space = z + 1 if direction == 0 else z - 1
        tm = t if k == 0 else partner
        slot = 2 * (1 + direction) + r
        return [
            copy(src, dst.at[slot], s_near.at[direction, k, i], r_q.at[slot, i], tm, space)
            for i, (src, dst) in enumerate(
                ((q_ref.at[head], qbuf), (g_ref.at[head], gbuf), (own_stat.at[head], stat))
            )
            if i in parts
        ]

    own_copies = [
        copy(q_ref.at[other], qbuf.at[r], s_own.at[0], r_q.at[r, 0], partner, z),
        copy(k_ref.at[other], kbuf.at[r], s_own.at[1], r_kv.at[r, 0], partner, z),
        copy(v_ref.at[other], vbuf.at[r], s_own.at[2], r_kv.at[r, 1], partner, z),
        copy(g_ref.at[other], gbuf.at[r], s_own.at[3], r_q.at[r, 1], partner, z),
        copy(own_stat.at[other], stat.at[r], s_own.at[4], r_q.at[r, 2], partner, z),
    ]

    def cross_copies():
        out = []
        for head in range(2):
            tm = member(head, 1 - group)
            out.append(copy(k_ref.at[head], kbuf.at[2], s_cross.at[head, 0], r_kv.at[2, 0], tm, z))
            out.append(copy(v_ref.at[head], vbuf.at[2], s_cross.at[head, 1], r_kv.at[2, 1], tm, z))
        return out

    for k in range(2):
        @pl.when(has_high)
        def _():
            for c in near_copies(0, k, (0, 1)):
                c.start()

        @pl.when(has_low)
        def _():
            for c in near_copies(1, k, (0, 1)):
                c.start()

        if k == 0:
            for c in own_copies[:4]:
                c.start()

            @pl.when(r == 1)
            def _():
                for c in cross_copies():
                    c.start()

    for c in local:
        c.wait()
    for head in range(2):
        prod = own_g[head].astype(jnp.float32) * own_o[head].astype(jnp.float32)
        own_stat[head, 0:1, :] = own_lse[head, 0, 0] * LOG2E
        own_stat[head, 1:2, :] = jnp.sum(prod.T, axis=0, keepdims=True)
    own_copies[4].start()
    for k in range(2):
        @pl.when(has_high)
        def _():
            near_copies(0, k, (2,))[0].start()

        @pl.when(has_low)
        def _():
            near_copies(1, k, (2,))[0].start()

    dq_acc[...] = jnp.zeros_like(dq_acc)
    dk_acc[...] = jnp.zeros_like(dk_acc)
    dv_acc[...] = jnp.zeros_like(dv_acc)
    stat[r] = own_stat[r]
    kt[r] = kbuf[r].T

    def pair(qs, ks):
        qb = qbuf[qs]
        gb = gbuf[qs]
        kb = kbuf[ks]
        vb = vbuf[ks]
        s = lax.dot_general(kb, qb, NT_DIMS, preferred_element_type=jnp.float32)
        p = jnp.exp2(s * (scale * LOG2E) - stat[qs, 0:1, :])
        dp = lax.dot_general(vb, gb, NT_DIMS, preferred_element_type=jnp.float32)
        ds = (p * (dp - stat[qs, 1:2, :])).astype(jnp.bfloat16)
        p = p.astype(jnp.bfloat16)
        dv_acc[ks] += jnp.dot(p, gb, preferred_element_type=jnp.float32)
        dk_acc[ks] += jnp.dot(ds, qb, preferred_element_type=jnp.float32)
        dq_acc[qs] += jnp.dot(kt[ks], ds, preferred_element_type=jnp.float32)

    def q_arrivals(slot):
        return [
            copy(q_ref.at[0], qbuf.at[slot], s_own.at[0], r_q.at[slot, 0], partner, z),
            copy(g_ref.at[0], gbuf.at[slot], s_own.at[0], r_q.at[slot, 1], partner, z),
            copy(own_stat.at[0], stat.at[slot], s_own.at[0], r_q.at[slot, 2], partner, z),
        ]

    def kv_arrivals(slot):
        return [
            copy(k_ref.at[0], kbuf.at[slot], s_own.at[0], r_kv.at[slot, 0], partner, z),
            copy(v_ref.at[0], vbuf.at[slot], s_own.at[0], r_kv.at[slot, 1], partner, z),
        ]

    @pl.loop(0, 4)
    def _(i):
        @pl.when(i == 1)
        def _():
            for c in q_arrivals(other) + kv_arrivals(other):
                c.wait_recv()
            kt[other] = kbuf[other].T

        pair(lax.rem(r + i // 2, 2), lax.rem(r + i, 2))

    for c in kv_arrivals(2):
        c.wait_recv()
    kt[2] = kbuf[2].T

    def dq_copy(slot, source, tm, space):
        return copy(
            dq_send.at[slot], dq_recv.at[r, source], s_dq.at[slot], r_dq.at[r, source], tm, space
        )

    def own_dq_copy():
        return dq_copy(other, 0, partner, z)

    def near_dq_copy(direction, role):
        space = z - 1 if direction == 0 else z + 1
        return dq_copy(2 * (1 + direction) + role, 2 - direction, member(role, group), space)

    def cross_dkv():
        return [
            copy(dk_send.at[2], dk_recv.at[r, 1], s_dkv.at[2, 0], r_dkv.at[r, 1, 0], inner_there, z),
            copy(dv_send.at[2], dv_recv.at[r, 1], s_dkv.at[2, 1], r_dkv.at[r, 1, 1], inner_there, z),
        ]

    def own_dkv():
        return [
            copy(dk_send.at[other], dk_recv.at[r, 0], s_dkv.at[other, 0], r_dkv.at[r, 0, 0], partner, z),
            copy(dv_send.at[other], dv_recv.at[r, 0], s_dkv.at[other, 1], r_dkv.at[r, 0, 1], partner, z),
        ]

    pair(1, 2)

    dq_send[other] = (dq_acc[other] * scale).astype(jnp.bfloat16)
    own_dq_copy().start()

    first = 1 - low_n
    last = 1 + high_n

    @pl.loop(0, 2)
    def _(step):
        role = lax.rem(r + step, 2)

        @pl.when(has_low)
        def _():
            for c in q_arrivals(2 + role):
                c.wait_recv()

        @pl.when(has_high)
        def _():
            for c in q_arrivals(4 + role):
                c.wait_recv()

        @pl.when(role == 1)
        def _():
            @pl.loop(first, last)
            def _(d):
                pair(2 * (1 + d) + 1, 2)

            dk_send[2] = (dk_acc[2] * scale).astype(jnp.bfloat16)
            dv_send[2] = dv_acc[2].astype(jnp.bfloat16)
            for c in cross_dkv():
                c.start()

        @pl.loop(2 * first, 2 * last)
        def _(i):
            d = i // 2
            slot = 2 * (1 + d) + role
            pair(slot, lax.rem(i, 2))

            @pl.when(lax.rem(i, 2) == 1)
            def _():
                dq_send[slot] = (dq_acc[slot] * scale).astype(jnp.bfloat16)

                @pl.when(d == 0)
                def _():
                    near_dq_copy(0, role).start()

                @pl.when(d == 1)
                def _():
                    near_dq_copy(1, role).start()

    dk_send[other] = (dk_acc[other] * scale).astype(jnp.bfloat16)
    dv_send[other] = dv_acc[other].astype(jnp.bfloat16)
    for c in own_dkv():
        c.start()

    def dq_arrival(head, source):
        return copy(
            dq_send.at[0], dq_recv.at[head, source], s_own.at[0], r_dq.at[head, source], partner, z
        )

    def dkv_arrivals(head, source):
        return [
            copy(dk_send.at[0], dk_recv.at[head, source], s_own.at[0], r_dkv.at[head, source, 0], partner, z),
            copy(dv_send.at[0], dv_recv.at[head, source], s_own.at[0], r_dkv.at[head, source, 1], partner, z),
        ]

    dk_mine = dk_acc[r] * scale
    dv_mine = dv_acc[r]

    @pl.when(r == 0)
    def _():
        gk_ref[r] = dk_mine.astype(gk_ref.dtype)
        gv_ref[r] = dv_mine.astype(gv_ref.dtype)
        for c in dkv_arrivals(other, 0):
            c.wait_recv()
        gk_ref[other] = dk_recv[other, 0]
        gv_ref[other] = dv_recv[other, 0]

    @pl.when(r == 1)
    def _():
        for c in dkv_arrivals(0, 1) + dkv_arrivals(1, 1):
            c.wait_recv()
        gk_ref[r] = (dk_mine + dk_recv[r, 1].astype(jnp.float32)).astype(gk_ref.dtype)
        gv_ref[r] = (dv_mine + dv_recv[r, 1].astype(jnp.float32)).astype(gv_ref.dtype)
        for c in dkv_arrivals(other, 0):
            c.wait_recv()
        for recv, out in ((dk_recv, gk_ref), (dv_recv, gv_ref)):
            out[other] = (
                recv[other, 0].astype(jnp.float32) + recv[other, 1].astype(jnp.float32)
            ).astype(out.dtype)

    dq_arrival(other, 0).wait_recv()
    totals = [dq_acc.at[r], dq_acc.at[other]]
    dq_acc[r] = dq_acc[r] * scale
    dq_acc[other] = dq_recv[other, 0].astype(jnp.float32)

    for source, there in ((1, has_low), (2, has_high)):
        @pl.when(there)
        def _():
            for head, total in ((r, totals[0]), (other, totals[1])):
                dq_arrival(head, source).wait_recv()
                total[...] += dq_recv[head, source].astype(jnp.float32)

    for head, total in ((r, totals[0]), (other, totals[1])):
        gq_ref[head] = total[...].T.astype(gq_ref.dtype)

    for c in own_copies + [own_dq_copy()] + cross_dkv() + own_dkv():
        c.wait_send()

    @pl.when(r == 1)
    def _():
        for c in cross_copies():
            c.wait_send()

    @pl.when(has_high)
    def _():
        for c in near_copies(0, 0) + near_copies(0, 1):
            c.wait_send()
        for role in range(2):
            near_dq_copy(1, role).wait_send()

    @pl.when(has_low)
    def _():
        for c in near_copies(1, 0) + near_copies(1, 1):
            c.wait_send()
        for role in range(2):
            near_dq_copy(0, role).wait_send()


def body(rows, query_tiles, key_tiles, value_tiles, out_tiles, grad_tiles, log_sum_exp):
    heads, _, _, columns, tile, dim = query_tiles.shape
    flat = (heads, tile, dim)
    bf, f32 = jnp.bfloat16, jnp.float32
    dma = pltpu.SemaphoreType.DMA
    grads = pl.pallas_call(
        functools.partial(kernel, rows),
        out_shape=jax.ShapeDtypeStruct((3,) + flat, bf),
        in_specs=[pl.BlockSpec(memory_space=pltpu.HBM)] * 6,
        out_specs=pl.BlockSpec(memory_space=pltpu.VMEM),
        scratch_shapes=[
            pltpu.VMEM((6, tile, dim), bf),
            pltpu.VMEM((6, tile, dim), bf),
            pltpu.VMEM((6, 2, tile), f32),
            pltpu.VMEM((3, tile, dim), bf),
            pltpu.VMEM((3, tile, dim), bf),
            pltpu.VMEM((3, dim, tile), bf),
            pltpu.VMEM(flat, bf),
            pltpu.VMEM(flat, bf),
            pltpu.VMEM((heads, 1, 1, 1, tile), f32),
            pltpu.VMEM((heads, 2, tile), f32),
            pltpu.VMEM((6, dim, tile), f32),
            pltpu.VMEM((3, tile, dim), f32),
            pltpu.VMEM((3, tile, dim), f32),
            pltpu.VMEM((6, dim, tile), bf),
            pltpu.VMEM((3, tile, dim), bf),
            pltpu.VMEM((3, tile, dim), bf),
            pltpu.VMEM((2, 3, dim, tile), bf),
            pltpu.VMEM((2, 2, tile, dim), bf),
            pltpu.VMEM((2, 2, tile, dim), bf),
            dma((7,)),
            dma((5,)),
            dma((2, 2, 3)),
            dma((2, 2)),
            dma((6,)),
            dma((3, 2)),
            dma((6, 3)),
            dma((3, 2)),
            dma((2, 3)),
            dma((2, 2, 2)),
        ],
        compiler_params=pltpu.CompilerParams(
            collective_id=0, has_side_effects=True, vmem_limit_bytes=60 * 2**20
        ),
        cost_estimate=pl.CostEstimate(
            flops=15 * 5 * 2 * tile * tile * dim,
            bytes_accessed=16 * tile * dim * 2,
            transcendentals=15 * tile * tile,
        ),
        name="tile_attention_backward",
    )(
        query_tiles.reshape(flat), key_tiles.reshape(flat), value_tiles.reshape(flat),
        out_tiles.reshape(flat), grad_tiles.reshape(flat), log_sum_exp,
    )
    outs = (grads[0], grads[1], grads[2])
    return tuple(o.reshape(query_tiles.shape) for o in outs)


def solution(mesh):
    tiles = P("head", "tm", "space", None, None, None)
    assert mesh.shape["tm"] == 4
    return jax.shard_map(
        functools.partial(body, mesh.shape["space"]),
        mesh=mesh,
        in_specs=(tiles,) * 5 + (P("head", "tm", "space", None, None),),
        out_specs=(tiles,) * 3,
        check_vma=False,
    )
```

```python
import functools
import math

import jax
import jax.numpy as jnp
from jax import lax
from jax.experimental import pallas as pl
from jax.experimental.pallas import tpu as pltpu
from jax.sharding import PartitionSpec as P


MESH = pl.DeviceIdType.MESH
LOG2E = math.log2(math.e)
NT_DIMS = (((1,), (1,)), ((), ()))


def member(role, group):
    return 2 * group + lax.rem(role + group, 2)


def kernel(
    rows,
    q_ref, k_ref, v_ref, o_ref, g_ref, lse_ref,
    grads_ref,
    qbuf, gbuf, stat, kbuf, vbuf, kt, own_g, own_o, own_lse, own_stat,
    dq_acc, dk_acc, dv_acc, dq_send, dk_send, dv_send, dq_recv, dk_recv, dv_recv,
    lsem, s_own, s_near, s_cross, s_dq, s_dkv, r_q, r_kv, r_dq, r_dkv,
):
    tile, dim = q_ref.shape[1:]
    scale = dim ** -0.5
    t = lax.axis_index("tm")
    z = lax.axis_index("space")
    group = t // 2
    r = lax.rem(t + group, 2)
    other = 1 - r
    partner = member(other, group)
    has_low = z > 0
    has_high = z < rows - 1
    inner_there = member(1, 1 - group)

    def copy(src, dst, ssem, rsem, tm, space):
        return pltpu.make_async_remote_copy(
            src_ref=src, dst_ref=dst, send_sem=ssem, recv_sem=rsem,
            device_id={"tm": tm, "space": space}, device_id_type=MESH,
        )

    gq_ref, gk_ref, gv_ref = (grads_ref.at[i] for i in range(3))
    barrier = pltpu.get_barrier_semaphore()

    def greet(tm, space):
        pl.semaphore_signal(
            barrier, inc=1, device_id={"tm": tm, "space": space}, device_id_type=MESH
        )

    greet(partner, z)
    greet(inner_there, z)

    @pl.when(r == 1)
    def _():
        greet(member(0, 1 - group), z)

    @pl.when(has_low)
    def _():
        greet(t, z - 1)
        greet(partner, z - 1)

    @pl.when(has_high)
    def _():
        greet(t, z + 1)
        greet(partner, z + 1)

    local = [
        pltpu.make_async_copy(q_ref.at[r], qbuf.at[r], lsem.at[0]),
        pltpu.make_async_copy(k_ref.at[r], kbuf.at[r], lsem.at[1]),
        pltpu.make_async_copy(v_ref.at[r], vbuf.at[r], lsem.at[2]),
        pltpu.make_async_copy(g_ref.at[r], gbuf.at[r], lsem.at[3]),
        pltpu.make_async_copy(g_ref, own_g, lsem.at[4]),
        pltpu.make_async_copy(o_ref, own_o, lsem.at[5]),
        pltpu.make_async_copy(lse_ref, own_lse, lsem.at[6]),
    ]
    for c in local:
        c.start()

    for c in local:
        c.wait()
    for head in range(2):
        prod = own_g[head].astype(jnp.float32) * own_o[head].astype(jnp.float32)
        own_stat[head, 0:1, :] = own_lse[head, 0, 0] * LOG2E
        own_stat[head, 1:2, :] = jnp.sum(prod.T, axis=0, keepdims=True)

    low_n = has_low.astype(jnp.int32)
    high_n = has_high.astype(jnp.int32)
    pl.semaphore_wait(barrier, 2 + r + 2 * low_n + 2 * high_n)

    def near_copies(direction, k):
        head = r if k == 0 else other
        space = z + 1 if direction == 0 else z - 1
        tm = t if k == 0 else partner
        slot = 2 * (1 + direction) + r
        return [
            copy(src, dst.at[slot], s_near.at[direction, k, i], r_q.at[slot, i], tm, space)
            for i, (src, dst) in enumerate(
                ((own_stat.at[head], stat), (q_ref.at[head], qbuf), (g_ref.at[head], gbuf))
            )
        ]

    own_copies = [
        copy(own_stat.at[other], stat.at[r], s_own.at[0], r_q.at[r, 0], partner, z),
        copy(q_ref.at[other], qbuf.at[r], s_own.at[1], r_q.at[r, 1], partner, z),
        copy(k_ref.at[other], kbuf.at[r], s_own.at[2], r_kv.at[r, 0], partner, z),
        copy(g_ref.at[other], gbuf.at[r], s_own.at[3], r_q.at[r, 2], partner, z),
        copy(v_ref.at[other], vbuf.at[r], s_own.at[4], r_kv.at[r, 1], partner, z),
    ]

    def cross_copies():
        out = []
        for head in range(2):
            tm = member(head, 1 - group)
            out.append(copy(k_ref.at[head], kbuf.at[2], s_cross.at[head, 0], r_kv.at[2, 0], tm, z))
            out.append(copy(v_ref.at[head], vbuf.at[2], s_cross.at[head, 1], r_kv.at[2, 1], tm, z))
        return out

    for c in own_copies:
        c.start()

    for k in range(2):
        @pl.when(has_high)
        def _():
            for c in near_copies(0, k):
                c.start()

        @pl.when(has_low)
        def _():
            for c in near_copies(1, k):
                c.start()

        if k == 0:
            @pl.when(r == 1)
            def _():
                for c in cross_copies():
                    c.start()

    dq_acc[...] = jnp.zeros_like(dq_acc)
    dk_acc[...] = jnp.zeros_like(dk_acc)
    dv_acc[...] = jnp.zeros_like(dv_acc)
    stat[r] = own_stat[r]
    kt[r] = kbuf[r].T

    def pair(qs, ks):
        qb = qbuf[qs]
        gb = gbuf[qs]
        kb = kbuf[ks]
        vb = vbuf[ks]
        s = lax.dot_general(kb, qb, NT_DIMS, preferred_element_type=jnp.float32)
        p = jnp.exp2(s * (scale * LOG2E) - stat[qs, 0:1, :])
        dp = lax.dot_general(vb, gb, NT_DIMS, preferred_element_type=jnp.float32)
        ds = (p * (dp - stat[qs, 1:2, :])).astype(jnp.bfloat16)
        p = p.astype(jnp.bfloat16)
        dv_acc[ks] += jnp.dot(p, gb, preferred_element_type=jnp.float32)
        dk_acc[ks] += jnp.dot(ds, qb, preferred_element_type=jnp.float32)
        dq_acc[qs] += jnp.dot(kt[ks], ds, preferred_element_type=jnp.float32)

    def q_arrivals(slot):
        return [
            copy(own_stat.at[0], stat.at[slot], s_own.at[0], r_q.at[slot, 0], partner, z),
            copy(q_ref.at[0], qbuf.at[slot], s_own.at[0], r_q.at[slot, 1], partner, z),
            copy(g_ref.at[0], gbuf.at[slot], s_own.at[0], r_q.at[slot, 2], partner, z),
        ]

    def kv_arrivals(slot):
        return [
            copy(k_ref.at[0], kbuf.at[slot], s_own.at[0], r_kv.at[slot, 0], partner, z),
            copy(v_ref.at[0], vbuf.at[slot], s_own.at[0], r_kv.at[slot, 1], partner, z),
        ]

    @pl.loop(0, 4)
    def _(i):
        @pl.when(i == 1)
        def _():
            for c in q_arrivals(other) + kv_arrivals(other):
                c.wait_recv()
            kt[other] = kbuf[other].T

        pair(lax.rem(r + i // 2, 2), lax.rem(r + i, 2))

    for c in kv_arrivals(2):
        c.wait_recv()
    kt[2] = kbuf[2].T

    def dq_copy(slot, source, tm, space):
        return copy(
            dq_send.at[slot], dq_recv.at[r, source], s_dq.at[slot], r_dq.at[r, source], tm, space
        )

    def own_dq_copy():
        return dq_copy(other, 0, partner, z)

    def near_dq_copy(direction, role):
        space = z - 1 if direction == 0 else z + 1
        return dq_copy(2 * (1 + direction) + role, 2 - direction, member(role, group), space)

    def cross_dkv():
        return [
            copy(dk_send.at[2], dk_recv.at[r, 1], s_dkv.at[2, 0], r_dkv.at[r, 1, 0], inner_there, z),
            copy(dv_send.at[2], dv_recv.at[r, 1], s_dkv.at[2, 1], r_dkv.at[r, 1, 1], inner_there, z),
        ]

    def own_dkv():
        return [
            copy(dk_send.at[other], dk_recv.at[r, 0], s_dkv.at[other, 0], r_dkv.at[r, 0, 0], partner, z),
            copy(dv_send.at[other], dv_recv.at[r, 0], s_dkv.at[other, 1], r_dkv.at[r, 0, 1], partner, z),
        ]

    pair(1, 2)

    dq_send[other] = (dq_acc[other] * scale).astype(jnp.bfloat16)
    own_dq_copy().start()

    first = 1 - low_n
    last = 1 + high_n

    @pl.loop(0, 2)
    def _(step):
        role = lax.rem(r + step, 2)

        @pl.when(has_low)
        def _():
            for c in q_arrivals(2 + role):
                c.wait_recv()

        @pl.when(has_high)
        def _():
            for c in q_arrivals(4 + role):
                c.wait_recv()

        @pl.when(role == 1)
        def _():
            @pl.loop(first, last)
            def _(d):
                pair(2 * (1 + d) + 1, 2)

            dk_send[2] = (dk_acc[2] * scale).astype(jnp.bfloat16)
            dv_send[2] = dv_acc[2].astype(jnp.bfloat16)
            for c in cross_dkv():
                c.start()

        @pl.loop(2 * first, 2 * last)
        def _(i):
            d = i // 2
            slot = 2 * (1 + d) + role
            pair(slot, lax.rem(i, 2))

            @pl.when(lax.rem(i, 2) == 1)
            def _():
                dq_send[slot] = (dq_acc[slot] * scale).astype(jnp.bfloat16)

                @pl.when(d == 0)
                def _():
                    near_dq_copy(0, role).start()

                @pl.when(d == 1)
                def _():
                    near_dq_copy(1, role).start()

    dk_send[other] = (dk_acc[other] * scale).astype(jnp.bfloat16)
    dv_send[other] = dv_acc[other].astype(jnp.bfloat16)
    for c in own_dkv():
        c.start()

    def dq_arrival(head, source):
        return copy(
            dq_send.at[0], dq_recv.at[head, source], s_own.at[0], r_dq.at[head, source], partner, z
        )

    def dkv_arrivals(head, source):
        return [
            copy(dk_send.at[0], dk_recv.at[head, source], s_own.at[0], r_dkv.at[head, source, 0], partner, z),
            copy(dv_send.at[0], dv_recv.at[head, source], s_own.at[0], r_dkv.at[head, source, 1], partner, z),
        ]

    dk_mine = dk_acc[r] * scale
    dv_mine = dv_acc[r]

    @pl.when(r == 0)
    def _():
        gk_ref[r] = dk_mine.astype(gk_ref.dtype)
        gv_ref[r] = dv_mine.astype(gv_ref.dtype)
        for c in dkv_arrivals(other, 0):
            c.wait_recv()
        gk_ref[other] = dk_recv[other, 0]
        gv_ref[other] = dv_recv[other, 0]

    @pl.when(r == 1)
    def _():
        for c in dkv_arrivals(0, 1) + dkv_arrivals(1, 1):
            c.wait_recv()
        gk_ref[r] = (dk_mine + dk_recv[r, 1].astype(jnp.float32)).astype(gk_ref.dtype)
        gv_ref[r] = (dv_mine + dv_recv[r, 1].astype(jnp.float32)).astype(gv_ref.dtype)
        for c in dkv_arrivals(other, 0):
            c.wait_recv()
        for recv, out in ((dk_recv, gk_ref), (dv_recv, gv_ref)):
            out[other] = (
                recv[other, 0].astype(jnp.float32) + recv[other, 1].astype(jnp.float32)
            ).astype(out.dtype)

    dq_arrival(other, 0).wait_recv()
    totals = [dq_acc.at[r], dq_acc.at[other]]
    dq_acc[r] = dq_acc[r] * scale
    dq_acc[other] = dq_recv[other, 0].astype(jnp.float32)

    for source, there in ((1, has_low), (2, has_high)):
        @pl.when(there)
        def _():
            for head, total in ((r, totals[0]), (other, totals[1])):
                dq_arrival(head, source).wait_recv()
                total[...] += dq_recv[head, source].astype(jnp.float32)

    for head, total in ((r, totals[0]), (other, totals[1])):
        gq_ref[head] = total[...].T.astype(gq_ref.dtype)

    for c in own_copies + [own_dq_copy()] + cross_dkv() + own_dkv():
        c.wait_send()

    @pl.when(r == 1)
    def _():
        for c in cross_copies():
            c.wait_send()

    @pl.when(has_high)
    def _():
        for c in near_copies(0, 0) + near_copies(0, 1):
            c.wait_send()
        for role in range(2):
            near_dq_copy(1, role).wait_send()

    @pl.when(has_low)
    def _():
        for c in near_copies(1, 0) + near_copies(1, 1):
            c.wait_send()
        for role in range(2):
            near_dq_copy(0, role).wait_send()


def body(rows, query_tiles, key_tiles, value_tiles, out_tiles, grad_tiles, log_sum_exp):
    heads, _, _, columns, tile, dim = query_tiles.shape
    flat = (heads, tile, dim)
    bf, f32 = jnp.bfloat16, jnp.float32
    dma = pltpu.SemaphoreType.DMA
    grads = pl.pallas_call(
        functools.partial(kernel, rows),
        out_shape=jax.ShapeDtypeStruct((3,) + flat, bf),
        in_specs=[pl.BlockSpec(memory_space=pltpu.HBM)] * 6,
        out_specs=pl.BlockSpec(memory_space=pltpu.VMEM),
        scratch_shapes=[
            pltpu.VMEM((6, tile, dim), bf),
            pltpu.VMEM((6, tile, dim), bf),
            pltpu.VMEM((6, 2, tile), f32),
            pltpu.VMEM((3, tile, dim), bf),
            pltpu.VMEM((3, tile, dim), bf),
            pltpu.VMEM((3, dim, tile), bf),
            pltpu.VMEM(flat, bf),
            pltpu.VMEM(flat, bf),
            pltpu.VMEM((heads, 1, 1, 1, tile), f32),
            pltpu.VMEM((heads, 2, tile), f32),
            pltpu.VMEM((6, dim, tile), f32),
            pltpu.VMEM((3, tile, dim), f32),
            pltpu.VMEM((3, tile, dim), f32),
            pltpu.VMEM((6, dim, tile), bf),
            pltpu.VMEM((3, tile, dim), bf),
            pltpu.VMEM((3, tile, dim), bf),
            pltpu.VMEM((2, 3, dim, tile), bf),
            pltpu.VMEM((2, 2, tile, dim), bf),
            pltpu.VMEM((2, 2, tile, dim), bf),
            dma((7,)),
            dma((5,)),
            dma((2, 2, 3)),
            dma((2, 2)),
            dma((6,)),
            dma((3, 2)),
            dma((6, 3)),
            dma((3, 2)),
            dma((2, 3)),
            dma((2, 2, 2)),
        ],
        compiler_params=pltpu.CompilerParams(
            collective_id=0, has_side_effects=True, vmem_limit_bytes=60 * 2**20
        ),
        cost_estimate=pl.CostEstimate(
            flops=15 * 5 * 2 * tile * tile * dim,
            bytes_accessed=16 * tile * dim * 2,
            transcendentals=15 * tile * tile,
        ),
        name="tile_attention_backward",
    )(
        query_tiles.reshape(flat), key_tiles.reshape(flat), value_tiles.reshape(flat),
        out_tiles.reshape(flat), grad_tiles.reshape(flat), log_sum_exp,
    )
    outs = (grads[0], grads[1], grads[2])
    return tuple(o.reshape(query_tiles.shape) for o in outs)


def solution(mesh):
    tiles = P("head", "tm", "space", None, None, None)
    assert mesh.shape["tm"] == 4
    return jax.shard_map(
        functools.partial(body, mesh.shape["space"]),
        mesh=mesh,
        in_specs=(tiles,) * 5 + (P("head", "tm", "space", None, None),),
        out_specs=(tiles,) * 3,
        check_vma=False,
    )
```

```python
import functools
import math

import jax
import jax.numpy as jnp
from jax import lax
from jax.experimental import pallas as pl
from jax.experimental.pallas import tpu as pltpu
from jax.sharding import PartitionSpec as P


MESH = pl.DeviceIdType.MESH
LOG2E = math.log2(math.e)
NT_DIMS = (((1,), (1,)), ((), ()))


def member(role, group):
    return 2 * group + lax.rem(role + group, 2)


def kernel(
    rows,
    q_ref, k_ref, v_ref, o_ref, g_ref, lse_ref,
    grads_ref,
    grads, qbuf, gbuf, stat, kbuf, vbuf, kt, own_g, own_o, own_lse, own_stat,
    dq_acc, dk_acc, dv_acc, dq_send, dk_send, dv_send, dq_recv, dk_recv, dv_recv,
    lsem, s_own, s_near, s_cross, s_dq, s_dkv, r_q, r_kv, r_dq, r_dkv, w_out,
):
    tile, dim = q_ref.shape[1:]
    scale = dim ** -0.5
    t = lax.axis_index("tm")
    z = lax.axis_index("space")
    group = t // 2
    r = lax.rem(t + group, 2)
    other = 1 - r
    partner = member(other, group)
    has_low = z > 0
    has_high = z < rows - 1
    inner_there = member(1, 1 - group)

    def copy(src, dst, ssem, rsem, tm, space):
        return pltpu.make_async_remote_copy(
            src_ref=src, dst_ref=dst, send_sem=ssem, recv_sem=rsem,
            device_id={"tm": tm, "space": space}, device_id_type=MESH,
        )

    gq_ref, gk_ref, gv_ref = (grads.at[i] for i in range(3))
    barrier = pltpu.get_barrier_semaphore()

    def greet(tm, space):
        pl.semaphore_signal(
            barrier, inc=1, device_id={"tm": tm, "space": space}, device_id_type=MESH
        )

    greet(partner, z)
    greet(inner_there, z)

    @pl.when(r == 1)
    def _():
        greet(member(0, 1 - group), z)

    @pl.when(has_low)
    def _():
        greet(t, z - 1)
        greet(partner, z - 1)

    @pl.when(has_high)
    def _():
        greet(t, z + 1)
        greet(partner, z + 1)

    local = [
        pltpu.make_async_copy(q_ref.at[r], qbuf.at[r], lsem.at[0]),
        pltpu.make_async_copy(k_ref.at[r], kbuf.at[r], lsem.at[1]),
        pltpu.make_async_copy(v_ref.at[r], vbuf.at[r], lsem.at[2]),
        pltpu.make_async_copy(g_ref.at[r], gbuf.at[r], lsem.at[3]),
        pltpu.make_async_copy(g_ref, own_g, lsem.at[4]),
        pltpu.make_async_copy(o_ref, own_o, lsem.at[5]),
        pltpu.make_async_copy(lse_ref, own_lse, lsem.at[6]),
    ]
    for c in local:
        c.start()

    for c in local:
        c.wait()
    for head in range(2):
        prod = own_g[head].astype(jnp.float32) * own_o[head].astype(jnp.float32)
        own_stat[head, 0:1, :] = own_lse[head, 0, 0] * LOG2E
        own_stat[head, 1:2, :] = jnp.sum(prod.T, axis=0, keepdims=True)

    low_n = has_low.astype(jnp.int32)
    high_n = has_high.astype(jnp.int32)
    pl.semaphore_wait(barrier, 2 + r + 2 * low_n + 2 * high_n)

    def near_copies(direction, k):
        head = r if k == 0 else other
        space = z + 1 if direction == 0 else z - 1
        tm = t if k == 0 else partner
        slot = 2 * (1 + direction) + r
        return [
            copy(src, dst.at[slot], s_near.at[direction, k, i], r_q.at[slot, i], tm, space)
            for i, (src, dst) in enumerate(
                ((own_stat.at[head], stat), (q_ref.at[head], qbuf), (g_ref.at[head], gbuf))
            )
        ]

    own_copies = [
        copy(own_stat.at[other], stat.at[r], s_own.at[0], r_q.at[r, 0], partner, z),
        copy(q_ref.at[other], qbuf.at[r], s_own.at[1], r_q.at[r, 1], partner, z),
        copy(k_ref.at[other], kbuf.at[r], s_own.at[2], r_kv.at[r, 0], partner, z),
        copy(g_ref.at[other], gbuf.at[r], s_own.at[3], r_q.at[r, 2], partner, z),
        copy(v_ref.at[other], vbuf.at[r], s_own.at[4], r_kv.at[r, 1], partner, z),
    ]

    def cross_copies():
        out = []
        for head in range(2):
            tm = member(head, 1 - group)
            out.append(copy(k_ref.at[head], kbuf.at[2], s_cross.at[head, 0], r_kv.at[2, 0], tm, z))
            out.append(copy(v_ref.at[head], vbuf.at[2], s_cross.at[head, 1], r_kv.at[2, 1], tm, z))
        return out

    for c in own_copies:
        c.start()

    for k in range(2):
        @pl.when(has_high)
        def _():
            for c in near_copies(0, k):
                c.start()

        @pl.when(has_low)
        def _():
            for c in near_copies(1, k):
                c.start()

        if k == 0:
            @pl.when(r == 1)
            def _():
                for c in cross_copies():
                    c.start()

    dq_acc[...] = jnp.zeros_like(dq_acc)
    dk_acc[...] = jnp.zeros_like(dk_acc)
    dv_acc[...] = jnp.zeros_like(dv_acc)
    stat[r] = own_stat[r]
    kt[r] = kbuf[r].T

    def pair(qs, ks):
        qb = qbuf[qs]
        gb = gbuf[qs]
        kb = kbuf[ks]
        vb = vbuf[ks]
        s = lax.dot_general(kb, qb, NT_DIMS, preferred_element_type=jnp.float32)
        p = jnp.exp2(s * (scale * LOG2E) - stat[qs, 0:1, :])
        dp = lax.dot_general(vb, gb, NT_DIMS, preferred_element_type=jnp.float32)
        ds = (p * (dp - stat[qs, 1:2, :])).astype(jnp.bfloat16)
        p = p.astype(jnp.bfloat16)
        dv_acc[ks] += jnp.dot(p, gb, preferred_element_type=jnp.float32)
        dk_acc[ks] += jnp.dot(ds, qb, preferred_element_type=jnp.float32)
        dq_acc[qs] += jnp.dot(kt[ks], ds, preferred_element_type=jnp.float32)

    def q_arrivals(slot):
        return [
            copy(own_stat.at[0], stat.at[slot], s_own.at[0], r_q.at[slot, 0], partner, z),
            copy(q_ref.at[0], qbuf.at[slot], s_own.at[0], r_q.at[slot, 1], partner, z),
            copy(g_ref.at[0], gbuf.at[slot], s_own.at[0], r_q.at[slot, 2], partner, z),
        ]

    def kv_arrivals(slot):
        return [
            copy(k_ref.at[0], kbuf.at[slot], s_own.at[0], r_kv.at[slot, 0], partner, z),
            copy(v_ref.at[0], vbuf.at[slot], s_own.at[0], r_kv.at[slot, 1], partner, z),
        ]

    @pl.loop(0, 4)
    def _(i):
        @pl.when(i == 1)
        def _():
            for c in q_arrivals(other) + kv_arrivals(other):
                c.wait_recv()
            kt[other] = kbuf[other].T

        pair(lax.rem(r + i // 2, 2), lax.rem(r + i, 2))

    for c in kv_arrivals(2):
        c.wait_recv()
    kt[2] = kbuf[2].T

    def dq_copy(slot, source, tm, space):
        return copy(
            dq_send.at[slot], dq_recv.at[r, source], s_dq.at[slot], r_dq.at[r, source], tm, space
        )

    def own_dq_copy():
        return dq_copy(other, 0, partner, z)

    def near_dq_copy(direction, role):
        space = z - 1 if direction == 0 else z + 1
        return dq_copy(2 * (1 + direction) + role, 2 - direction, member(role, group), space)

    def cross_dkv():
        return [
            copy(dk_send.at[2], dk_recv.at[r, 1], s_dkv.at[2, 0], r_dkv.at[r, 1, 0], inner_there, z),
            copy(dv_send.at[2], dv_recv.at[r, 1], s_dkv.at[2, 1], r_dkv.at[r, 1, 1], inner_there, z),
        ]

    def own_dkv():
        return [
            copy(dk_send.at[other], dk_recv.at[r, 0], s_dkv.at[other, 0], r_dkv.at[r, 0, 0], partner, z),
            copy(dv_send.at[other], dv_recv.at[r, 0], s_dkv.at[other, 1], r_dkv.at[r, 0, 1], partner, z),
        ]

    pair(1, 2)

    dq_send[other] = (dq_acc[other] * scale).astype(jnp.bfloat16)
    own_dq_copy().start()

    first = 1 - low_n
    last = 1 + high_n

    @pl.loop(0, 2)
    def _(step):
        role = lax.rem(r + step, 2)

        @pl.when(has_low)
        def _():
            for c in q_arrivals(2 + role):
                c.wait_recv()

        @pl.when(has_high)
        def _():
            for c in q_arrivals(4 + role):
                c.wait_recv()

        @pl.when(role == 1)
        def _():
            @pl.loop(first, last)
            def _(d):
                pair(2 * (1 + d) + 1, 2)

            dk_send[2] = (dk_acc[2] * scale).astype(jnp.bfloat16)
            dv_send[2] = dv_acc[2].astype(jnp.bfloat16)
            for c in cross_dkv():
                c.start()

        @pl.loop(2 * first, 2 * last)
        def _(i):
            d = i // 2
            slot = 2 * (1 + d) + role
            pair(slot, lax.rem(i, 2))

            @pl.when(lax.rem(i, 2) == 1)
            def _():
                dq_send[slot] = (dq_acc[slot] * scale).astype(jnp.bfloat16)

                @pl.when(d == 0)
                def _():
                    near_dq_copy(0, role).start()

                @pl.when(d == 1)
                def _():
                    near_dq_copy(1, role).start()

    dk_send[other] = (dk_acc[other] * scale).astype(jnp.bfloat16)
    dv_send[other] = dv_acc[other].astype(jnp.bfloat16)
    for c in own_dkv():
        c.start()

    def dq_arrival(head, source):
        return copy(
            dq_send.at[0], dq_recv.at[head, source], s_own.at[0], r_dq.at[head, source], partner, z
        )

    def dkv_arrivals(head, source):
        return [
            copy(dk_send.at[0], dk_recv.at[head, source], s_own.at[0], r_dkv.at[head, source, 0], partner, z),
            copy(dv_send.at[0], dv_recv.at[head, source], s_own.at[0], r_dkv.at[head, source, 1], partner, z),
        ]

    def write(i, head):
        return pltpu.make_async_copy(grads.at[i, head], grads_ref.at[i, head], w_out.at[i, head])

    dk_mine = dk_acc[r] * scale
    dv_mine = dv_acc[r]

    @pl.when(r == 0)
    def _():
        gk_ref[r] = dk_mine.astype(gk_ref.dtype)
        gv_ref[r] = dv_mine.astype(gv_ref.dtype)
        write(1, r).start()
        write(2, r).start()
        for c in dkv_arrivals(other, 0):
            c.wait_recv()
        gk_ref[other] = dk_recv[other, 0]
        gv_ref[other] = dv_recv[other, 0]
        write(1, other).start()
        write(2, other).start()

    @pl.when(r == 1)
    def _():
        for c in dkv_arrivals(0, 1) + dkv_arrivals(1, 1):
            c.wait_recv()
        gk_ref[r] = (dk_mine + dk_recv[r, 1].astype(jnp.float32)).astype(gk_ref.dtype)
        gv_ref[r] = (dv_mine + dv_recv[r, 1].astype(jnp.float32)).astype(gv_ref.dtype)
        write(1, r).start()
        write(2, r).start()
        for c in dkv_arrivals(other, 0):
            c.wait_recv()
        for recv, out in ((dk_recv, gk_ref), (dv_recv, gv_ref)):
            out[other] = (
                recv[other, 0].astype(jnp.float32) + recv[other, 1].astype(jnp.float32)
            ).astype(out.dtype)
        write(1, other).start()
        write(2, other).start()

    dq_arrival(other, 0).wait_recv()
    totals = [dq_acc.at[r], dq_acc.at[other]]
    dq_acc[r] = dq_acc[r] * scale
    dq_acc[other] = dq_recv[other, 0].astype(jnp.float32)

    for source, there in ((1, has_low), (2, has_high)):
        @pl.when(there)
        def _():
            for head, total in ((r, totals[0]), (other, totals[1])):
                dq_arrival(head, source).wait_recv()
                total[...] += dq_recv[head, source].astype(jnp.float32)

    for head, total in ((r, totals[0]), (other, totals[1])):
        gq_ref[head] = total[...].T.astype(gq_ref.dtype)
        write(0, head).start()

    for c in own_copies + [own_dq_copy()] + cross_dkv() + own_dkv():
        c.wait_send()

    @pl.when(r == 1)
    def _():
        for c in cross_copies():
            c.wait_send()

    @pl.when(has_high)
    def _():
        for c in near_copies(0, 0) + near_copies(0, 1):
            c.wait_send()
        for role in range(2):
            near_dq_copy(1, role).wait_send()

    @pl.when(has_low)
    def _():
        for c in near_copies(1, 0) + near_copies(1, 1):
            c.wait_send()
        for role in range(2):
            near_dq_copy(0, role).wait_send()

    for i in range(3):
        for head in range(2):
            write(i, head).wait()


def body(rows, query_tiles, key_tiles, value_tiles, out_tiles, grad_tiles, log_sum_exp):
    heads, _, _, columns, tile, dim = query_tiles.shape
    flat = (heads, tile, dim)
    bf, f32 = jnp.bfloat16, jnp.float32
    dma = pltpu.SemaphoreType.DMA
    grads = pl.pallas_call(
        functools.partial(kernel, rows),
        out_shape=jax.ShapeDtypeStruct((3,) + flat, bf),
        in_specs=[pl.BlockSpec(memory_space=pltpu.HBM)] * 6,
        out_specs=pl.BlockSpec(memory_space=pltpu.HBM),
        scratch_shapes=[
            pltpu.VMEM((3,) + flat, bf),
            pltpu.VMEM((6, tile, dim), bf),
            pltpu.VMEM((6, tile, dim), bf),
            pltpu.VMEM((6, 2, tile), f32),
            pltpu.VMEM((3, tile, dim), bf),
            pltpu.VMEM((3, tile, dim), bf),
            pltpu.VMEM((3, dim, tile), bf),
            pltpu.VMEM(flat, bf),
            pltpu.VMEM(flat, bf),
            pltpu.VMEM((heads, 1, 1, 1, tile), f32),
            pltpu.VMEM((heads, 2, tile), f32),
            pltpu.VMEM((6, dim, tile), f32),
            pltpu.VMEM((3, tile, dim), f32),
            pltpu.VMEM((3, tile, dim), f32),
            pltpu.VMEM((6, dim, tile), bf),
            pltpu.VMEM((3, tile, dim), bf),
            pltpu.VMEM((3, tile, dim), bf),
            pltpu.VMEM((2, 3, dim, tile), bf),
            pltpu.VMEM((2, 2, tile, dim), bf),
            pltpu.VMEM((2, 2, tile, dim), bf),
            dma((7,)),
            dma((5,)),
            dma((2, 2, 3)),
            dma((2, 2)),
            dma((6,)),
            dma((3, 2)),
            dma((6, 3)),
            dma((3, 2)),
            dma((2, 3)),
            dma((2, 2, 2)),
            dma((3, heads)),
        ],
        compiler_params=pltpu.CompilerParams(
            collective_id=0, has_side_effects=True, vmem_limit_bytes=60 * 2**20
        ),
        cost_estimate=pl.CostEstimate(
            flops=15 * 5 * 2 * tile * tile * dim,
            bytes_accessed=16 * tile * dim * 2,
            transcendentals=15 * tile * tile,
        ),
        name="tile_attention_backward",
    )(
        query_tiles.reshape(flat), key_tiles.reshape(flat), value_tiles.reshape(flat),
        out_tiles.reshape(flat), grad_tiles.reshape(flat), log_sum_exp,
    )
    outs = (grads[0], grads[1], grads[2])
    return tuple(o.reshape(query_tiles.shape) for o in outs)


def solution(mesh):
    tiles = P("head", "tm", "space", None, None, None)
    assert mesh.shape["tm"] == 4
    return jax.shard_map(
        functools.partial(body, mesh.shape["space"]),
        mesh=mesh,
        in_specs=(tiles,) * 5 + (P("head", "tm", "space", None, None),),
        out_specs=(tiles,) * 3,
        check_vma=False,
    )
```
